512 devices in a mesh: dp: 32 (over z, x), tensor: 16 (over y, core).
Axes of the slice: x: 4, y: 8, z: 8, core: 2. Of those that a mesh axis runs over, the one named last changes fastest.
Arguments:
- tokens: bfloat16 [12288, 1792], P('dp', 'tensor'), may hold values from -6 to 6
- cotangent: bfloat16 [12288, 1792], P('dp', 'tensor'), may hold values from -6 to 6
- gate_weight: bfloat16 [1792, 8192], P('dp', 'tensor'), may hold values from -0.125 to 0.125
- up_weight: bfloat16 [1792, 8192], P('dp', 'tensor'), may hold values from -0.125 to 0.125
- down_weight: bfloat16 [8192, 1792], P('tensor', 'dp'), may hold values from -0.0625 to 0.0625
- error_buffer: bfloat16 [32, 8192, 1792], P('dp', 'tensor'), may hold values from -803.4326 to 803.4326
- q_init: float32 [8, 1792], replicated, may hold values from -6 to 6
Outputs:
- grad_tokens: bfloat16 [12288, 1792], P('dp', 'tensor')
- new_error: bfloat16 [32, 8192, 1792], P('dp', 'tensor')
- q_avg: float32 [8, 1792], replicated
The draws below stay inside these ranges and needn't reach their ends.
All inputs are finite; a program needn't handle non-finite values.
Results may differ from the reference program's by a relative error of at most 0.0049.
Values may be sent and summed in bfloat16 or wider, within the bound.
No kernel may reach another device: no remote copies, remote signals or barrier semaphores. Data moves between devices by JAX's collectives and lax.ppermute only.
A program may use at most 64 MiB of HBM per device.

```python
import math
import jax
import jax.numpy as jnp
from jax import lax

D = 1792
FF = 8192
RANK = 8
TOK_DEV = 384
GROUPS = 32
TOKENS = 12288


def draw_error_buffer(key, part):
    key = jax.random.fold_in(key, 7)
    key_base, key_rows, key_cols, key_left, key_right, key_sizes, key_coef = jax.random.split(key, 7)
    rising = 3.0 ** (jnp.arange(FF, dtype=jnp.float32) / FF)
    base = jnp.clip(jax.random.normal(key_base, (GROUPS, FF, D), jnp.float32), -4.0, 4.0)
    row_scale = rising * jnp.exp(jax.random.uniform(key_rows, (FF,), jnp.float32, 0.0, math.log(4.0)))
    col_scale = jnp.exp(jax.random.uniform(key_cols, (D,), jnp.float32, 0.0, math.log(3.0)))
    left = jnp.clip(jax.random.normal(key_left, (FF, RANK), jnp.float32), -3.0, 3.0)
    right = jnp.clip(jax.random.normal(key_right, (D, RANK), jnp.float32), -3.0, 3.0)
    sizes = jnp.exp(jax.random.uniform(key_sizes, (RANK,), jnp.float32, 0.0, math.log(3.0)))
    growth = 3.0 ** (jnp.arange(GROUPS, dtype=jnp.float32) / GROUPS)
    spread = jnp.clip(jax.random.normal(key_coef, (GROUPS, RANK), jnp.float32), -3.0, 3.0)
    coef = sizes[None, :] + 0.25 * growth[:, None] * spread
    shared = jnp.zeros((GROUPS, FF, D), jnp.float32)
    for index in range(RANK):
        outer = left[:, index][:, None] * right[:, index][None, :]
        shared = shared + coef[:, index][:, None, None] * outer[None, :, :]
    value = base + 0.55 * shared
    scaled = value * (0.15 * math.sqrt(TOK_DEV)) * row_scale[None, :, None] * col_scale[None, None, :]
    limit = 40.0 * math.sqrt(TOK_DEV)
    return jnp.clip(scaled, -limit, limit).astype(jnp.bfloat16)


def levels(key, shape, pieces, least, top_value):
    def one(dim, blocks):
        heights = jax.random.uniform(jax.random.fold_in(jax.random.fold_in(key, 6), dim), (blocks,), jnp.float32, least / len(pieces), top_value / len(pieces))
        return jnp.repeat(jnp.exp(heights), shape[dim] // blocks).reshape((-1,) + (1,) * (len(shape) - dim - 1))

    gain = one(*pieces[0])
    for cut in pieces[1:]:
        gain = gain * one(*cut)
    return gain


def scatter_about(key, shape, scale, bound, cuts=(), kind=jnp.bfloat16):
    gain = levels(key, shape, cuts, -0.22, 0.18) if cuts else 1.0
    values = jax.random.normal(key, shape, jnp.float32) * scale * gain
    return jnp.minimum(jnp.maximum(values, -bound), bound).astype(kind)


def setup_inputs(seed: int = 0) -> dict:
    seeds = jax.random.split(jax.random.key(seed), 8)
    return {
        "tokens": scatter_about(seeds[0], (TOKENS, D), 1.0, 6.0, ((0, 32), (1, 16))),
        "cotangent": scatter_about(seeds[1], (TOKENS, D), 1.0, 6.0, ((0, 32), (1, 16))),
        "gate_weight": scatter_about(seeds[2], (D, FF), D ** -0.5, 0.125, ((0, 32), (1, 16))),
        "up_weight": scatter_about(seeds[3], (D, FF), D ** -0.5, 0.125, ((0, 32), (1, 16))),
        "down_weight": scatter_about(seeds[4], (FF, D), FF ** -0.5, 0.0625, ((0, 16), (1, 32))),
        "error_buffer": draw_error_buffer(jax.random.fold_in(seeds[7], 71), 0),
        "q_init": scatter_about(seeds[6], (RANK, D), 1.0, 6.0, (), jnp.float32),
    }


cubic_term = 0.044715
tanh_scale = math.sqrt(2.0 / math.pi)
highest = lax.Precision.HIGHEST

def gelu_parts(values):
    inner = tanh_scale * (values + cubic_term * values * values * values)
    tanh_val = jnp.tanh(inner)
    active = 0.5 * values * (1.0 + tanh_val)
    slope = 0.5 * (1.0 + tanh_val) + 0.5 * values * (1.0 - tanh_val * tanh_val) * tanh_scale * (1.0 + 3.0 * cubic_term * values * values)
    return (active, slope)

def orthonormal_rows(matrix):
    row_list = [matrix[position] for position in range(matrix.shape[0])]
    for position in range(len(row_list)):
        current = row_list[position]
        length = jnp.sqrt(jnp.dot(current, current, precision=highest))
        unit_row = current / length
        for later in range(position + 1, len(row_list)):
            weight_val = jnp.dot(row_list[later], unit_row, precision=highest)
            row_list[later] = row_list[later] - weight_val * unit_row
        row_list[position] = unit_row
    return jnp.stack(row_list)

def reference(tokens, cotangent, gate_weight, up_weight, down_weight, error_buffer, q_init):
    token_blocks = tokens.reshape(GROUPS, TOK_DEV, D)
    cot_blocks = cotangent.reshape(GROUPS, TOK_DEV, D)

    def group_pass(pair):
        inputs, upstream = pair
        gate = jnp.dot(inputs, gate_weight, preferred_element_type=jnp.float32)
        up_val = jnp.dot(inputs, up_weight, preferred_element_type=jnp.float32)
        active, slope = gelu_parts(gate)
        hidden = (active * up_val).astype(jnp.bfloat16)
        d_hidden = lax.dot_general(upstream, down_weight, (((1,), (1,)), ((), ())), preferred_element_type=jnp.float32)
        d_gate = (d_hidden * up_val * slope).astype(jnp.bfloat16)
        d_up = (d_hidden * active).astype(jnp.bfloat16)
        back = lax.dot_general(d_gate, gate_weight, (((1,), (1,)), ((), ())), preferred_element_type=jnp.float32)
        back = back + lax.dot_general(d_up, up_weight, (((1,), (1,)), ((), ())), preferred_element_type=jnp.float32)
        return (back.astype(jnp.bfloat16), hidden)
    grads, hiddens = lax.map(group_pass, (token_blocks, cot_blocks))
    grad_tokens = grads.reshape(TOKENS, D)

    def merged_of(hidden, upstream, errors):
        local_grad = lax.dot_general(hidden, upstream, (((0,), (0,)), ((), ())), preferred_element_type=jnp.float32)
        return local_grad + errors.astype(jnp.float32)

    def add_p(total, triple):
        merged = merged_of(*triple)
        term = lax.dot_general(q_init, merged, (((1,), (1,)), ((), ())), precision=highest, preferred_element_type=jnp.float32)
        return (total + term, None)
    p_sum, _ = lax.scan(add_p, jnp.zeros((RANK, FF), jnp.float32), (hiddens, cot_blocks, error_buffer))
    p_orth = orthonormal_rows(p_sum)

    def add_q(total, triple):
        merged = merged_of(*triple)
        return (total + jnp.dot(p_orth, merged, precision=highest, preferred_element_type=jnp.float32), None)
    q_sum, _ = lax.scan(add_q, jnp.zeros((RANK, D), jnp.float32), (hiddens, cot_blocks, error_buffer))
    q_avg = q_sum / GROUPS

    def new_block(triple):
        merged = merged_of(*triple)
        approx = lax.dot_general(p_orth, q_avg, (((0,), (0,)), ((), ())), precision=highest, preferred_element_type=jnp.float32)
        return (merged - approx).astype(jnp.bfloat16)
    new_error = lax.map(new_block, (hiddens, cot_blocks, error_buffer))
    return (grad_tokens, new_error, q_avg)
```

```python
import math

import jax
import jax.numpy as jnp
from jax import lax
from jax.experimental import pallas as pl
from jax.experimental.pallas import tpu as pltpu
from jax.sharding import Mesh, PartitionSpec as P

cubic_term = 0.044715
tanh_scale = math.sqrt(2.0 / math.pi)
bf16 = jnp.bfloat16
f32 = jnp.float32

Z, X, Y, C = 8, 4, 8, 2
SIZE = {"z": Z, "x": X, "y": Y, "c": C}
RANK = 8
LANES = 128


def gelu_parts(values):
    inner = tanh_scale * (values + cubic_term * values * values * values)
    tanh_val = jnp.tanh(inner)
    active = 0.5 * values * (1.0 + tanh_val)
    slope = 0.5 * (1.0 + tanh_val) + 0.5 * values * (1.0 - tanh_val * tanh_val) * tanh_scale * (
        1.0 + 3.0 * cubic_term * values * values
    )
    return (active, slope)


def contract(left, right, dim_left, dim_right):
    return lax.dot_general(
        left, right, (((dim_left,), (dim_right,)), ((), ())), preferred_element_type=f32
    )


def shift(value, axis, step):
    n = SIZE[axis]
    return lax.ppermute(value, axis, [(i, (i + step) % n) for i in range(n)])


def swap(stacked, axes):
    return lax.all_to_all(stacked, axes, 0, 0, tiled=True)


def gather(value, axes):
    n = math.prod(SIZE[a] for a in axes)
    return swap(jnp.broadcast_to(value[None], (n,) + value.shape), axes)


def pieces(value):
    first = lax.reduce_precision(value, 8, 7)
    rest = value - first
    second = lax.reduce_precision(rest, 8, 7)
    third = rest - second
    return first.astype(bf16), second.astype(bf16), third.astype(bf16)


def stack3(value):
    return jnp.concatenate(pieces(value), axis=0)


def fold3(value):
    n = value.shape[0] // 3
    return value[:n] + (value[n : 2 * n] + value[2 * n :])


def orth_kernel(mine, parts, orth, transform, rows):
    blocks, _, width = parts.shape
    width = width - LANES
    for t in range(blocks):
        rows[:, t * width : (t + 1) * width] = parts[t, :, LANES:]
    number = lax.broadcasted_iota(jnp.int32, (RANK, 1), 0)
    column = lax.broadcasted_iota(jnp.int32, (RANK, LANES), 1)
    trans = jnp.where(column == number, 1.0, 0.0).astype(f32)
    for j in range(RANK):
        whole = rows[...]
        row = whole[j : j + 1, :]
        products = jnp.sum(whole * row, axis=1, keepdims=True)
        length = jnp.sqrt(products[j : j + 1, :])
        unit = row / length
        weight = jnp.where(number > j, products / length, 0.0)
        rows[...] = jnp.where(number == j, unit, whole - weight * unit)
        unit_trans = trans[j : j + 1, :] / length
        trans = jnp.where(number == j, unit_trans, trans - weight * unit_trans)
    transform[...] = trans
    at = pl.multiple_of(mine[0] * width, LANES)
    orth[...] = rows[:, pl.ds(at, width)]


def orthonormal(parts, mine):
    blocks, _, width = parts.shape
    width = width - LANES
    return pl.pallas_call(
        orth_kernel,
        out_shape=(
            jax.ShapeDtypeStruct((RANK, width), f32),
            jax.ShapeDtypeStruct((RANK, LANES), f32),
        ),
        in_specs=[
            pl.BlockSpec(memory_space=pltpu.SMEM),
            pl.BlockSpec(memory_space=pltpu.VMEM),
        ],
        out_specs=(
            pl.BlockSpec(memory_space=pltpu.VMEM),
            pl.BlockSpec(memory_space=pltpu.VMEM),
        ),
        scratch_shapes=[pltpu.VMEM((RANK, blocks * width), f32)],
        compiler_params=pltpu.CompilerParams(vmem_limit_bytes=16 * 1024 * 1024),
    )(mine, parts)


def per_device(tokens, cotangent, gate_weight, up_weight, down_weight, error_buffer, q_init):
    y_at = lax.axis_index("y")
    c_at = lax.axis_index("c")
    errors = error_buffer[0]
    units = gate_weight.shape[1]

    pair = swap(jnp.stack([tokens.T, cotangent.T]), ("c",))
    block = pair.reshape(-1, pair.shape[-1])
    far = shift(block, "y", 4)
    back2 = shift(block, "y", 2)
    fore2 = shift(block, "y", -2)
    both = jnp.stack([block, far])
    back = shift(both, "y", 1)
    fore = shift(both, "y", -1)
    in_turn = jnp.stack([block, fore[0], fore2, back[1], far, fore[1], back2, back[0]])
    twice = jnp.concatenate([in_turn, in_turn], axis=0)
    ordered = lax.dynamic_slice_in_dim(twice, (Y - y_at) % Y, Y, axis=0)
    inputs, upstream = gather(ordered.reshape(-1, block.shape[-1]), ("c",))

    side = gather(jnp.stack([up_weight, down_weight.T]), ("x",))
    up_all = lax.all_gather(side[:, 0].reshape(-1, units), "z", axis=0, tiled=True)
    down_all = lax.all_gather(side[:, 1].reshape(-1, units), "z", axis=0, tiled=True)
    gate_z = gather(gate_weight, ("z",))
    gate_all = gather(gate_z, ("x",)).transpose(1, 0, 2, 3).reshape(-1, units)

    gate = contract(gate_all, inputs, 0, 0)
    up_val = contract(up_all, inputs, 0, 0)
    active, slope = gelu_parts(gate)
    hidden = (active * up_val).astype(bf16)

    q_stack = stack3(q_init)
    cot_q = stack3(fold3(contract(q_stack, upstream, 1, 0)))
    err_q = fold3(contract(q_stack, errors, 1, 1))
    p_part = fold3(contract(cot_q, hidden, 1, 1)) + err_q
    p_sum = jnp.sum(gather(p_part, ("z", "x")), axis=0)

    p_stack = stack3(p_sum)
    hid_p = stack3(fold3(contract(p_stack, hidden, 1, 0)))
    q_part = fold3(contract(p_stack, errors, 1, 0)) + fold3(contract(hid_p, upstream, 1, 1))
    tiles = q_part.reshape(RANK, -1, LANES).transpose(1, 0, 2)
    n_tiles = tiles.shape[0]
    tiles = jnp.concatenate([tiles, jnp.zeros((Y * C - n_tiles,) + tiles.shape[1:], f32)])
    message = jnp.concatenate(
        [tiles, jnp.broadcast_to(p_sum[None], (Y * C,) + p_sum.shape)], axis=2
    )
    parts = swap(message, ("y", "c"))
    q_tile = jnp.sum(parts[:, :, :LANES], axis=0)
    p_orth, trans = orthonormal(parts, (y_at * C + c_at).astype(jnp.int32).reshape(1))
    q_tile = jnp.sum(gather(q_tile, ("z", "x")), axis=0)
    q_tile = jnp.dot(trans[:, :RANK], q_tile, precision=lax.Precision.HIGHEST) / (Z * X)
    q_avg = gather(q_tile, ("y", "c"))[:n_tiles].transpose(1, 0, 2).reshape(RANK, -1)

    p1, p2, p3 = pieces(p_orth)
    q1, q2, q3 = pieces(q_avg)
    approx = contract(
        jnp.concatenate([p1, p1, p2, p2, p1, p3]),
        jnp.concatenate([q1, q2, q1, q2, q3, q1]),
        0,
        0,
    )
    local_grad = contract(hidden, upstream, 1, 1)
    new_error = (local_grad + errors.astype(f32) - approx).astype(bf16)[None]

    d_hidden = contract(down_all, upstream, 0, 0)
    d_gate = (d_hidden * up_val * slope).astype(bf16)
    d_up = (d_hidden * active).astype(bf16)
    grads = contract(gate_all, d_gate, 1, 0) + contract(up_all, d_up, 1, 0)
    grads = grads.reshape(Y, C, -1, grads.shape[-1])
    keep = jnp.where(c_at == 0, grads[:, 0], grads[:, 1])
    give = jnp.where(c_at == 0, grads[:, 1], grads[:, 0])
    chip = keep + shift(give, "c", 1)
    grad_tokens = lax.psum_scatter(chip, "y", scatter_dimension=0, tiled=False)
    return (grad_tokens.astype(bf16).T, new_error, q_avg)


def solution(mesh):
    fine = Mesh(mesh.devices.reshape(Z, X, Y, C), ("z", "x", "y", "c"))
    dp, tensor = ("z", "x"), ("y", "c")
    return jax.shard_map(
        per_device,
        mesh=fine,
        in_specs=(
            P(dp, tensor),
            P(dp, tensor),
            P(dp, tensor),
            P(dp, tensor),
            P(tensor, dp),
            P(dp, tensor, None),
            P(),
        ),
        out_specs=(P(dp, tensor), P(dp, tensor, None), P()),
        check_vma=False,
    )
```

```python
import math

import jax
import jax.numpy as jnp
from jax import lax
from jax.experimental import pallas as pl
from jax.experimental.pallas import tpu as pltpu
from jax.sharding import Mesh, PartitionSpec as P

cubic_term = 0.044715
tanh_scale = math.sqrt(2.0 / math.pi)
bf16 = jnp.bfloat16
f32 = jnp.float32

Z, X, Y, C = 8, 4, 8, 2
SIZE = {"z": Z, "x": X, "y": Y, "c": C}
RANK = 8
LANES = 128


def gelu_parts(values):
    inner = tanh_scale * (values + cubic_term * values * values * values)
    tanh_val = jnp.tanh(inner)
    active = 0.5 * values * (1.0 + tanh_val)
    slope = 0.5 * (1.0 + tanh_val) + 0.5 * values * (1.0 - tanh_val * tanh_val) * tanh_scale * (
        1.0 + 3.0 * cubic_term * values * values
    )
    return (active, slope)


def contract(left, right, dim_left, dim_right):
    return lax.dot_general(
        left, right, (((dim_left,), (dim_right,)), ((), ())), preferred_element_type=f32
    )


def shift(value, axis, step):
    n = SIZE[axis]
    return lax.ppermute(value, axis, [(i, (i + step) % n) for i in range(n)])


def swap(stacked, axes):
    return lax.all_to_all(stacked, axes, 0, 0, tiled=True)


def gather(value, axes):
    n = math.prod(SIZE[a] for a in axes)
    return swap(jnp.broadcast_to(value[None], (n,) + value.shape), axes)


def pieces(value):
    first = lax.reduce_precision(value, 8, 7)
    rest = value - first
    second = lax.reduce_precision(rest, 8, 7)
    third = rest - second
    return first.astype(bf16), second.astype(bf16), third.astype(bf16)


def stack3(value):
    return jnp.concatenate(pieces(value), axis=0)


def fold3(value):
    n = value.shape[0] // 3
    return value[:n] + (value[n : 2 * n] + value[2 * n :])


def place_kernel(count, plan, at, *refs):
    blocks, out = refs[:-1], refs[-1]
    rows = out.shape[1]
    for index, part, offset in plan:
        slot = lax.rem(at[0] + offset, count)
        if part == "top":
            out[slot, : rows // 2, :] = blocks[index][...]
        elif part == "end":
            out[slot, rows // 2 :, :] = blocks[index][...]
        elif part is None:
            out[slot] = blocks[index][...]
        else:
            out[slot] = blocks[index][part]


def place(blocks, plan, count, at):
    return pl.pallas_call(
        lambda *refs: place_kernel(count, plan, *refs),
        out_shape=jax.ShapeDtypeStruct((count,) + blocks[0].shape, blocks[0].dtype),
        in_specs=[pl.BlockSpec(memory_space=pltpu.SMEM)]
        + [pl.BlockSpec(memory_space=pltpu.VMEM)] * len(blocks),
        out_specs=pl.BlockSpec(memory_space=pltpu.VMEM),
        compiler_params=pltpu.CompilerParams(vmem_limit_bytes=24 * 1024 * 1024),
        name="place",
    )(at.astype(jnp.int32).reshape(1), *blocks)


def orth_kernel(mine, parts, orth, transform, rows):
    blocks, _, width = parts.shape
    width = width - LANES
    for t in range(blocks):
        rows[:, t * width : (t + 1) * width] = parts[t, :, LANES:]
    number = lax.broadcasted_iota(jnp.int32, (RANK, 1), 0)
    column = lax.broadcasted_iota(jnp.int32, (RANK, LANES), 1)
    trans = jnp.where(column == number, 1.0, 0.0).astype(f32)
    for j in range(RANK):
        whole = rows[...]
        row = whole[j : j + 1, :]
        products = jnp.sum(whole * row, axis=1, keepdims=True)
        length = jnp.sqrt(products[j : j + 1, :])
        unit = row / length
        weight = jnp.where(number > j, products / length, 0.0)
        rows[...] = jnp.where(number == j, unit, whole - weight * unit)
        unit_trans = trans[j : j + 1, :] / length
        trans = jnp.where(number == j, unit_trans, trans - weight * unit_trans)
    transform[...] = trans
    at = pl.multiple_of(mine[0] * width, LANES)
    orth[...] = rows[:, pl.ds(at, width)]


def orthonormal(parts, mine):
    blocks, _, width = parts.shape
    width = width - LANES
    return pl.pallas_call(
        orth_kernel,
        out_shape=(
            jax.ShapeDtypeStruct((RANK, width), f32),
            jax.ShapeDtypeStruct((RANK, LANES), f32),
        ),
        in_specs=[
            pl.BlockSpec(memory_space=pltpu.SMEM),
            pl.BlockSpec(memory_space=pltpu.VMEM),
        ],
        out_specs=(
            pl.BlockSpec(memory_space=pltpu.VMEM),
            pl.BlockSpec(memory_space=pltpu.VMEM),
        ),
        scratch_shapes=[pltpu.VMEM((RANK, blocks * width), f32)],
        compiler_params=pltpu.CompilerParams(vmem_limit_bytes=16 * 1024 * 1024),
    )(mine, parts)


def grad_share(d_hidden, up_val, slope, active, weights):
    d_gate = (d_hidden * up_val * slope).astype(bf16)
    d_up = (d_hidden * active).astype(bf16)
    grads = contract(weights, jnp.concatenate([d_gate, d_up]), 1, 0)
    return grads


def pass_kernel(value, _, out):
    out[...] = value[...]


def when_ready(value, other):
    return pl.pallas_call(
        pass_kernel,
        out_shape=jax.ShapeDtypeStruct(value.shape, value.dtype),
        in_specs=[pl.BlockSpec(memory_space=pltpu.VMEM), pl.BlockSpec(memory_space=pl.ANY)],
        out_specs=pl.BlockSpec(memory_space=pltpu.VMEM),
        name="when_ready",
    )(value, other)


def per_device(tokens, cotangent, gate_weight, up_weight, down_weight, error_buffer, q_init):
    x_at = lax.axis_index("x")
    y_at = lax.axis_index("y")
    c_at = lax.axis_index("c")
    errors = error_buffer[0]
    units = gate_weight.shape[1]

    first = c_at == 0

    both_weights = jnp.concatenate([gate_weight, up_weight], axis=1)
    weights_x = gather(both_weights, ("x",)).reshape(-1, 2 * units)
    weights_x, block, down = lax.optimization_barrier(
        (weights_x, jnp.stack([tokens.T, cotangent.T]), down_weight.T)
    )
    weights = lax.all_gather(weights_x, "z", axis=0, tiled=True)

    down_z = gather(down, ("z",)).reshape(-1, units)
    far = shift(block, "y", 4)
    back2 = shift(block, "y", 2)
    fore2 = shift(block, "y", -2)
    down_z, block, far = lax.optimization_barrier((down_z, block, far))
    down_all = gather(down_z, ("x",))
    both = jnp.stack([block, far])
    back = shift(both, "y", 1)
    fore = shift(both, "y", -1)
    mine = place(
        [block, far, back2, fore2, back, fore],
        [(0, None, 0), (1, None, 4), (2, None, 6), (3, None, 2), (4, 0, 7), (4, 1, 3), (5, 0, 1), (5, 1, 5)],
        Y,
        y_at,
    )
    mine, down_all = lax.optimization_barrier((mine, down_all))
    other = shift(mine, "c", 1)
    even = jnp.where(first, mine, other)
    odd = jnp.where(first, other, mine)
    inputs, upstream = (
        jnp.stack([even[:, kind], odd[:, kind]], axis=1).reshape(-1, block.shape[-1])
        for kind in (0, 1)
    )
    gate_up = contract(weights, inputs, 0, 0)
    gate, up_val = gate_up[:units], gate_up[units:]
    active, slope = gelu_parts(gate)
    hidden = (active * up_val).astype(bf16)
    hidden, down_all = lax.optimization_barrier((hidden, down_all))
    down_all = down_all.reshape(X, Z, -1, units).transpose(1, 0, 2, 3).reshape(-1, units)
    d_hidden = contract(down_all, upstream, 0, 0)

    q_stack = stack3(q_init)
    cot_q = stack3(fold3(contract(q_stack, upstream, 1, 0)))
    err_q = fold3(contract(q_stack, errors, 1, 1))
    p_part = fold3(contract(cot_q, hidden, 1, 1)) + err_q
    p_all = gather(p_part, ("z", "x"))
    grads = grad_share(d_hidden, up_val, slope, active, weights)
    p_sum = when_ready(jnp.sum(p_all, axis=0), grads)

    p_stack = stack3(p_sum)
    hid_p = stack3(fold3(contract(p_stack, hidden, 1, 0)))
    q_part = fold3(contract(p_stack, errors, 1, 0)) + fold3(contract(hid_p, upstream, 1, 1))
    tiles = q_part.reshape(RANK, -1, LANES).transpose(1, 0, 2)
    n_tiles = tiles.shape[0]
    tiles = jnp.concatenate([tiles, jnp.zeros((Y * C - n_tiles,) + tiles.shape[1:], f32)])
    message = jnp.concatenate(
        [tiles, jnp.broadcast_to(p_sum[None], (Y * C,) + p_sum.shape)], axis=2
    )
    parts = swap(message, ("y", "c"))
    q_tile = jnp.sum(parts[:, :, :LANES], axis=0)
    p_orth, trans = orthonormal(parts, (y_at * C + c_at).astype(jnp.int32).reshape(1))
    q_tile = jnp.sum(gather(q_tile, ("z", "x")), axis=0)
    q_tile = jnp.dot(trans[:, :RANK], q_tile, precision=lax.Precision.HIGHEST) / (Z * X)
    q_avg = gather(q_tile, ("y", "c"))[:n_tiles].transpose(1, 0, 2).reshape(RANK, -1)

    p1, p2, p3 = pieces(p_orth)
    q1, q2, q3 = pieces(q_avg)
    approx = contract(
        jnp.concatenate([p1, p1, p2, p2, p1, p3]),
        jnp.concatenate([q1, q2, q1, q2, q3, q1]),
        0,
        0,
    )
    local_grad = contract(hidden, upstream, 1, 1)
    new_error = (local_grad + errors.astype(f32) - approx).astype(bf16)[None]

    grad_tokens = lax.psum_scatter(grads, ("y", "c"), scatter_dimension=0, tiled=True)
    return (grad_tokens.astype(bf16).T, new_error, q_avg)


def solution(mesh):
    fine = Mesh(mesh.devices.reshape(Z, X, Y, C), ("z", "x", "y", "c"))
    dp, tensor = ("z", "x"), ("y", "c")
    return jax.shard_map(
        per_device,
        mesh=fine,
        in_specs=(
            P(dp, tensor),
            P(dp, tensor),
            P(dp, tensor),
            P(dp, tensor),
            P(tensor, dp),
            P(dp, tensor, None),
            P(),
        ),
        out_specs=(P(dp, tensor), P(dp, tensor, None), P()),
        check_vma=False,
    )
```

```python
import math

import jax
import jax.numpy as jnp
from jax import lax
from jax.experimental import pallas as pl
from jax.experimental.pallas import tpu as pltpu
from jax.sharding import Mesh, PartitionSpec as P

cubic_term = 0.044715
tanh_scale = math.sqrt(2.0 / math.pi)
bf16 = jnp.bfloat16
f32 = jnp.float32

Z, X, Y, C = 8, 4, 8, 2
SIZE = {"z": Z, "x": X, "y": Y, "c": C}
RANK = 8
LANES = 128


def gelu_parts(values):
    inner = tanh_scale * (values + cubic_term * values * values * values)
    tanh_val = jnp.tanh(inner)
    active = 0.5 * values * (1.0 + tanh_val)
    slope = 0.5 * (1.0 + tanh_val) + 0.5 * values * (1.0 - tanh_val * tanh_val) * tanh_scale * (
        1.0 + 3.0 * cubic_term * values * values
    )
    return (active, slope)


def contract(left, right, dim_left, dim_right):
    return lax.dot_general(
        left, right, (((dim_left,), (dim_right,)), ((), ())), preferred_element_type=f32
    )


def shift(value, axis, step):
    n = SIZE[axis]
    return lax.ppermute(value, axis, [(i, (i + step) % n) for i in range(n)])


def swap(stacked, axes):
    return lax.all_to_all(stacked, axes, 0, 0, tiled=True)


def gather(value, axes):
    n = math.prod(SIZE[a] for a in axes)
    return swap(jnp.broadcast_to(value[None], (n,) + value.shape), axes)


def pieces(value):
    first = lax.reduce_precision(value, 8, 7)
    rest = value - first
    second = lax.reduce_precision(rest, 8, 7)
    third = rest - second
    return first.astype(bf16), second.astype(bf16), third.astype(bf16)


def stack3(value):
    return jnp.concatenate(pieces(value), axis=0)


def fold3(value):
    n = value.shape[0] // 3
    return value[:n] + (value[n : 2 * n] + value[2 * n :])


def place_kernel(count, plan, at, *refs):
    blocks, out = refs[:-1], refs[-1]
    rows = out.shape[1]
    for index, part, offset in plan:
        slot = lax.rem(at[0] + offset, count)
        if part == "top":
            out[slot, : rows // 2, :] = blocks[index][...]
        elif part == "end":
            out[slot, rows // 2 :, :] = blocks[index][...]
        elif part is None:
            out[slot] = blocks[index][...]
        else:
            out[slot] = blocks[index][part]


def place(blocks, plan, count, at):
    return pl.pallas_call(
        lambda *refs: place_kernel(count, plan, *refs),
        out_shape=jax.ShapeDtypeStruct((count,) + blocks[0].shape, blocks[0].dtype),
        in_specs=[pl.BlockSpec(memory_space=pltpu.SMEM)]
        + [pl.BlockSpec(memory_space=pltpu.VMEM)] * len(blocks),
        out_specs=pl.BlockSpec(memory_space=pltpu.VMEM),
        compiler_params=pltpu.CompilerParams(vmem_limit_bytes=24 * 1024 * 1024),
        name="place",
    )(at.astype(jnp.int32).reshape(1), *blocks)


def triangle_kernel(p_sum, _, out):
    rows = p_sum[...]
    number = lax.broadcasted_iota(jnp.int32, (RANK, 1), 0)
    lane = lax.broadcasted_iota(jnp.int32, (RANK, LANES), 1)
    factor = jnp.zeros((RANK, LANES), f32)
    for j in range(RANK):
        row = rows[j : j + 1, :]
        products = jnp.sum(rows * row, axis=1, keepdims=True)
        length = jnp.sqrt(products[j : j + 1, :])
        some = length > 0.0
        scale = jnp.where(some, 1.0 / jnp.where(some, length, 1.0), 0.0)
        unit = row * scale
        weight = jnp.where(number > j, products * scale, 0.0)
        column = jnp.where(number == j, length, weight)
        factor = jnp.where(lane == j, column, factor)
        rows = rows - weight * unit
    out[...] = factor


def triangle(p_sum, later):
    return pl.pallas_call(
        triangle_kernel,
        out_shape=jax.ShapeDtypeStruct((RANK, LANES), f32),
        in_specs=[pl.BlockSpec(memory_space=pltpu.VMEM), pl.BlockSpec(memory_space=pl.ANY)],
        out_specs=pl.BlockSpec(memory_space=pltpu.VMEM),
        name="triangle",
    )(p_sum, later)


def split3(value):
    first = value.astype(bf16)
    rest = value - first.astype(f32)
    second = rest.astype(bf16)
    third = (rest - second.astype(f32)).astype(bf16)
    return first, second, third


def finish_kernel(parts, p_sum, q_avg, left, right):
    blocks = parts.shape[0]
    tiles = q_avg.shape[1] // LANES
    rows = [parts[t, :, LANES:] for t in range(blocks)]
    number = lax.broadcasted_iota(jnp.int32, (RANK, 1), 0)
    column = lax.broadcasted_iota(jnp.int32, (RANK, LANES), 1)
    trans = jnp.where(column == number, 1.0, 0.0).astype(f32)
    for j in range(RANK):
        each = [block * block[j : j + 1, :] for block in rows]
        while len(each) > 1:
            each = [one + two for one, two in zip(each[::2], each[1::2])]
        products = jnp.sum(each[0], axis=1, keepdims=True)
        length = jnp.sqrt(products[j : j + 1, :])
        weight = jnp.where(number > j, products / length, 0.0)
        rows = [block - weight * (block[j : j + 1, :] / length) for block in rows]
        unit = trans[j : j + 1, :] / length
        trans = jnp.where(number == j, unit, trans - weight * unit)

    def apply(value):
        total = trans[:, 0:1] * value[0:1, :]
        for i in range(1, RANK):
            total = total + trans[:, i : i + 1] * value[i : i + 1, :]
        return total

    l1, l2, l3 = split3(apply(p_sum[...]))
    for at, piece in enumerate((l1, l1, l2, l2, l1, l3)):
        left[at] = piece
    for t in range(tiles):
        here = slice(t * LANES, (t + 1) * LANES)
        average = apply(parts[t, :, :LANES]) / (Z * X)
        q_avg[:, here] = average
        r1, r2, r3 = split3(average)
        for at, piece in enumerate((r1, r2, r1, r2, r3, r1)):
            right[at, :, here] = piece


def finish(parts, p_sum, width):
    return pl.pallas_call(
        finish_kernel,
        out_shape=(
            jax.ShapeDtypeStruct((RANK, width), f32),
            jax.ShapeDtypeStruct((6, RANK, p_sum.shape[1]), bf16),
            jax.ShapeDtypeStruct((6, RANK, width), bf16),
        ),
        cost_estimate=pl.CostEstimate(
            flops=40_000_000_000, bytes_accessed=130_000_000, transcendentals=0
        ),
        name="finish",
    )(parts, p_sum)


def grad_share(d_hidden, up_val, slope, active, weights):
    d_gate = (d_hidden * up_val * slope).astype(bf16)
    d_up = (d_hidden * active).astype(bf16)
    grads = contract(weights, jnp.concatenate([d_gate, d_up]), 1, 0)
    return grads


def per_device(tokens, cotangent, gate_weight, up_weight, down_weight, error_buffer, q_init):
    x_at = lax.axis_index("x")
    y_at = lax.axis_index("y")
    c_at = lax.axis_index("c")
    errors = error_buffer[0]
    units = gate_weight.shape[1]

    first = c_at == 0

    both_weights = jnp.concatenate([gate_weight, up_weight], axis=1)
    weights_x = gather(both_weights, ("x",)).reshape(-1, 2 * units)
    weights_x, block, down = lax.optimization_barrier(
        (weights_x, jnp.stack([tokens.T, cotangent.T]), down_weight.T)
    )
    weights = lax.all_gather(weights_x, "z", axis=0, tiled=True)

    down_z = gather(down, ("z",)).reshape(-1, units)
    far = shift(block, "y", 4)
    back2 = shift(block, "y", 2)
    fore2 = shift(block, "y", -2)
    down_z, block, far = lax.optimization_barrier((down_z, block, far))
    down_all = gather(down_z, ("x",))
    both = jnp.stack([block, far])
    back = shift(both, "y", 1)
    fore = shift(both, "y", -1)
    mine = place(
        [block, far, back2, fore2, back, fore],
        [(0, None, 0), (1, None, 4), (2, None, 6), (3, None, 2), (4, 0, 7), (4, 1, 3), (5, 0, 1), (5, 1, 5)],
        Y,
        y_at,
    )
    mine, down_all = lax.optimization_barrier((mine, down_all))
    other = shift(mine, "c", 1)
    even = jnp.where(first, mine, other)
    odd = jnp.where(first, other, mine)
    inputs, upstream = (
        jnp.stack([even[:, kind], odd[:, kind]], axis=1).reshape(-1, block.shape[-1])
        for kind in (0, 1)
    )
    gate_up = contract(weights, inputs, 0, 0)
    gate, up_val = gate_up[:units], gate_up[units:]
    active, slope = gelu_parts(gate)
    hidden = (active * up_val).astype(bf16)
    hidden, down_all = lax.optimization_barrier((hidden, down_all))
    down_all = down_all.reshape(X, Z, -1, units).transpose(1, 0, 2, 3).reshape(-1, units)
    d_hidden = contract(down_all, upstream, 0, 0)

    q_stack = stack3(q_init)
    cot_q = stack3(fold3(contract(q_stack, upstream, 1, 0)))
    err_q = fold3(contract(q_stack, errors, 1, 1))
    p_part = fold3(contract(cot_q, hidden, 1, 1)) + err_q
    p_all = gather(p_part, ("z", "x"))
    grads = grad_share(d_hidden, up_val, slope, active, weights)
    p_all, shares = lax.optimization_barrier((p_all, grads))
    p_sum = jnp.sum(p_all, axis=0)

    p_stack = stack3(p_sum)
    hid_p = stack3(fold3(contract(p_stack, hidden, 1, 0)))
    q_part = fold3(contract(p_stack, errors, 1, 0)) + fold3(contract(hid_p, upstream, 1, 1))
    tiles = q_part.reshape(RANK, -1, LANES).transpose(1, 0, 2)
    n_tiles = tiles.shape[0]
    tiles = jnp.concatenate([tiles, jnp.zeros((Y * C - n_tiles,) + tiles.shape[1:], f32)])
    q_tile = jnp.sum(swap(tiles, ("y", "c")), axis=0)
    q_tile = jnp.sum(gather(q_tile, ("z", "x")), axis=0)
    ends = gather(jnp.concatenate([q_tile, triangle(p_sum, shares)], axis=1), ("y", "c"))
    q_avg, left, right = finish(ends, p_sum, errors.shape[1])
    approx = lax.dot_general(
        left, right, (((0, 1), (0, 1)), ((), ())), preferred_element_type=f32
    )
    local_grad = contract(hidden, upstream, 1, 1)
    new_error = (local_grad + errors.astype(f32) - approx).astype(bf16)[None]

    grad_tokens = lax.psum_scatter(grads, ("y", "c"), scatter_dimension=0, tiled=True)
    return (grad_tokens.astype(bf16).T, new_error, q_avg)


def solution(mesh):
    fine = Mesh(mesh.devices.reshape(Z, X, Y, C), ("z", "x", "y", "c"))
    dp, tensor = ("z", "x"), ("y", "c")
    return jax.shard_map(
        per_device,
        mesh=fine,
        in_specs=(
            P(dp, tensor),
            P(dp, tensor),
            P(dp, tensor),
            P(dp, tensor),
            P(tensor, dp),
            P(dp, tensor, None),
            P(),
        ),
        out_specs=(P(dp, tensor), P(dp, tensor, None), P()),
        check_vma=False,
    )
```

```python
import math

import jax
import jax.numpy as jnp
from jax import lax
from jax.experimental import pallas as pl
from jax.experimental.pallas import tpu as pltpu
from jax.sharding import Mesh, PartitionSpec as P

cubic_term = 0.044715
tanh_scale = math.sqrt(2.0 / math.pi)
bf16 = jnp.bfloat16
f32 = jnp.float32

Z, X, Y, C = 8, 4, 8, 2
SIZE = {"z": Z, "x": X, "y": Y, "c": C}
RANK = 8
LANES = 128


def gelu_parts(values):
    inner = tanh_scale * (values + cubic_term * values * values * values)
    tanh_val = jnp.tanh(inner)
    active = 0.5 * values * (1.0 + tanh_val)
    slope = 0.5 * (1.0 + tanh_val) + 0.5 * values * (1.0 - tanh_val * tanh_val) * tanh_scale * (
        1.0 + 3.0 * cubic_term * values * values
    )
    return (active, slope)


def contract(left, right, dim_left, dim_right):
    return lax.dot_general(
        left, right, (((dim_left,), (dim_right,)), ((), ())), preferred_element_type=f32
    )


def shift(value, axis, step):
    n = SIZE[axis]
    return lax.ppermute(value, axis, [(i, (i + step) % n) for i in range(n)])


def swap(stacked, axes):
    return lax.all_to_all(stacked, axes, 0, 0, tiled=True)


def gather(value, axes):
    n = math.prod(SIZE[a] for a in axes)
    return swap(jnp.broadcast_to(value[None], (n,) + value.shape), axes)


def pieces(value):
    first = lax.reduce_precision(value, 8, 7)
    rest = value - first
    second = lax.reduce_precision(rest, 8, 7)
    third = rest - second
    return first.astype(bf16), second.astype(bf16), third.astype(bf16)


def stack3(value):
    return jnp.concatenate(pieces(value), axis=0)


def fold3(value):
    n = value.shape[0] // 3
    return value[:n] + (value[n : 2 * n] + value[2 * n :])


def place_kernel(count, plan, at, *refs):
    blocks, out = refs[:-1], refs[-1]
    rows = out.shape[1]
    for index, part, offset in plan:
        slot = lax.rem(at[0] + offset, count)
        if part == "top":
            out[slot, : rows // 2, :] = blocks[index][...]
        elif part == "end":
            out[slot, rows // 2 :, :] = blocks[index][...]
        elif part is None:
            out[slot] = blocks[index][...]
        else:
            out[slot] = blocks[index][part]


def place(blocks, plan, count, at):
    return pl.pallas_call(
        lambda *refs: place_kernel(count, plan, *refs),
        out_shape=jax.ShapeDtypeStruct((count,) + blocks[0].shape, blocks[0].dtype),
        in_specs=[pl.BlockSpec(memory_space=pltpu.SMEM)]
        + [pl.BlockSpec(memory_space=pltpu.VMEM)] * len(blocks),
        out_specs=pl.BlockSpec(memory_space=pltpu.VMEM),
        compiler_params=pltpu.CompilerParams(vmem_limit_bytes=24 * 1024 * 1024),
        name="place",
    )(at.astype(jnp.int32).reshape(1), *blocks)


def triangle_kernel(p_sum, _, out):
    rows = p_sum[...]
    number = lax.broadcasted_iota(jnp.int32, (RANK, 1), 0)
    lane = lax.broadcasted_iota(jnp.int32, (RANK, LANES), 1)
    factor = jnp.zeros((RANK, LANES), f32)
    for j in range(RANK):
        row = rows[j : j + 1, :]
        products = jnp.sum(rows * row, axis=1, keepdims=True)
        length = jnp.sqrt(products[j : j + 1, :])
        some = length > 0.0
        scale = jnp.where(some, 1.0 / jnp.where(some, length, 1.0), 0.0)
        unit = row * scale
        weight = jnp.where(number > j, products * scale, 0.0)
        column = jnp.where(number == j, length, weight)
        factor = jnp.where(lane == j, column, factor)
        rows = rows - weight * unit
    out[...] = factor


def triangle(p_sum, later):
    return pl.pallas_call(
        triangle_kernel,
        out_shape=jax.ShapeDtypeStruct((RANK, LANES), f32),
        in_specs=[pl.BlockSpec(memory_space=pltpu.VMEM), pl.BlockSpec(memory_space=pl.ANY)],
        out_specs=pl.BlockSpec(memory_space=pltpu.VMEM),
        name="triangle",
    )(p_sum, later)


def split3(value):
    first = value.astype(bf16)
    rest = value - first.astype(f32)
    second = rest.astype(bf16)
    third = (rest - second.astype(f32)).astype(bf16)
    return first, second, third


def finish_kernel(parts, p_sum, q_avg, left, right):
    blocks = parts.shape[0]
    tiles = q_avg.shape[1] // LANES
    rows = [parts[t, :, LANES:] for t in range(blocks)]
    number = lax.broadcasted_iota(jnp.int32, (RANK, 1), 0)
    column = lax.broadcasted_iota(jnp.int32, (RANK, LANES), 1)
    trans = jnp.where(column == number, 1.0, 0.0).astype(f32)
    for j in range(RANK):
        each = [block * block[j : j + 1, :] for block in rows]
        while len(each) > 1:
            each = [one + two for one, two in zip(each[::2], each[1::2])]
        products = jnp.sum(each[0], axis=1, keepdims=True)
        length = jnp.sqrt(products[j : j + 1, :])
        weight = jnp.where(number > j, products / length, 0.0)
        rows = [block - weight * (block[j : j + 1, :] / length) for block in rows]
        unit = trans[j : j + 1, :] / length
        trans = jnp.where(number == j, unit, trans - weight * unit)

    def apply(value):
        total = trans[:, 0:1] * value[0:1, :]
        for i in range(1, RANK):
            total = total + trans[:, i : i + 1] * value[i : i + 1, :]
        return total

    l1, l2, l3 = split3(apply(p_sum[...]))
    for at, piece in enumerate((l1, l1, l2, l2, l1, l3)):
        left[at] = piece
    for t in range(tiles):
        here = slice(t * LANES, (t + 1) * LANES)
        average = apply(parts[t, :, :LANES]) / (Z * X)
        q_avg[:, here] = average
        r1, r2, r3 = split3(average)
        for at, piece in enumerate((r1, r2, r1, r2, r3, r1)):
            right[at, :, here] = piece


def finish(parts, p_sum, width):
    return pl.pallas_call(
        finish_kernel,
        out_shape=(
            jax.ShapeDtypeStruct((RANK, width), f32),
            jax.ShapeDtypeStruct((6, RANK, p_sum.shape[1]), bf16),
            jax.ShapeDtypeStruct((6, RANK, width), bf16),
        ),
        cost_estimate=pl.CostEstimate(
            flops=40_000_000_000, bytes_accessed=130_000_000, transcendentals=0
        ),
        name="finish",
    )(parts, p_sum)


def grad_share(d_hidden, up_val, slope, active, weights):
    d_gate = (d_hidden * up_val * slope).astype(bf16)
    d_up = (d_hidden * active).astype(bf16)
    grads = contract(weights, jnp.concatenate([d_gate, d_up]), 1, 0)
    return grads


def per_device(tokens, cotangent, gate_weight, up_weight, down_weight, error_buffer, q_init):
    x_at = lax.axis_index("x")
    y_at = lax.axis_index("y")
    c_at = lax.axis_index("c")
    errors = error_buffer[0]
    units = gate_weight.shape[1]

    first = c_at == 0

    both_weights = jnp.concatenate([gate_weight, up_weight], axis=1)
    weights_x = gather(both_weights, ("x",)).reshape(-1, 2 * units)
    weights_x, block, down = lax.optimization_barrier(
        (weights_x, jnp.stack([tokens.T, cotangent.T]), down_weight.T)
    )
    weights = lax.all_gather(weights_x, "z", axis=0, tiled=True)

    down_z = gather(down, ("z",)).reshape(-1, units)
    far = shift(block, "y", 4)
    back2 = shift(block, "y", 2)
    fore2 = shift(block, "y", -2)
    down_z, block, far, back2, fore2 = lax.optimization_barrier((down_z, block, far, back2, fore2))
    down_all = gather(down_z, ("x",))
    both = jnp.stack([block, far])
    back = shift(both, "y", 1)
    fore = shift(both, "y", -1)
    mine = place(
        [block, far, back2, fore2, back, fore],
        [(0, None, 0), (1, None, 4), (2, None, 6), (3, None, 2), (4, 0, 7), (4, 1, 3), (5, 0, 1), (5, 1, 5)],
        Y,
        y_at,
    )
    other = shift(mine, "c", 1)
    even = jnp.where(first, mine, other)
    odd = jnp.where(first, other, mine)
    inputs, upstream = (
        jnp.stack([even[:, kind], odd[:, kind]], axis=1).reshape(-1, block.shape[-1])
        for kind in (0, 1)
    )
    gate_up = contract(weights, inputs, 0, 0)
    gate, up_val = gate_up[:units], gate_up[units:]
    active, slope = gelu_parts(gate)
    hidden = (active * up_val).astype(bf16)
    hidden, down_all = lax.optimization_barrier((hidden, down_all))
    down_all = down_all.reshape(X, Z, -1, units).transpose(1, 0, 2, 3).reshape(-1, units)
    d_hidden = contract(down_all, upstream, 0, 0)

    q_stack = stack3(q_init)
    cot_q = stack3(fold3(contract(q_stack, upstream, 1, 0)))
    err_q = fold3(contract(q_stack, errors, 1, 1))
    p_part = fold3(contract(cot_q, hidden, 1, 1)) + err_q
    p_all = gather(p_part, ("z", "x"))
    grads = grad_share(d_hidden, up_val, slope, active, weights)
    p_all, shares = lax.optimization_barrier((p_all, grads))
    p_sum = jnp.sum(p_all, axis=0)

    p_stack = stack3(p_sum)
    hid_p = stack3(fold3(contract(p_stack, hidden, 1, 0)))
    q_part = fold3(contract(p_stack, errors, 1, 0)) + fold3(contract(hid_p, upstream, 1, 1))
    tiles = q_part.reshape(RANK, -1, LANES).transpose(1, 0, 2)
    n_tiles = tiles.shape[0]
    tiles = jnp.concatenate([tiles, jnp.zeros((Y * C - n_tiles,) + tiles.shape[1:], f32)])
    q_tile = jnp.sum(swap(tiles, ("y", "c")), axis=0)
    q_tile = jnp.sum(gather(q_tile, ("z", "x")), axis=0)
    ends = gather(jnp.concatenate([q_tile, triangle(p_sum, shares)], axis=1), ("y", "c"))
    q_avg, left, right = finish(ends, p_sum, errors.shape[1])
    approx = lax.dot_general(
        left, right, (((0, 1), (0, 1)), ((), ())), preferred_element_type=f32
    )
    local_grad = contract(hidden, upstream, 1, 1)
    new_error = (local_grad + errors.astype(f32) - approx).astype(bf16)[None]

    grad_tokens = lax.psum_scatter(grads, ("y", "c"), scatter_dimension=0, tiled=True)
    return (grad_tokens.astype(bf16).T, new_error, q_avg)


def solution(mesh):
    fine = Mesh(mesh.devices.reshape(Z, X, Y, C), ("z", "x", "y", "c"))
    dp, tensor = ("z", "x"), ("y", "c")
    return jax.shard_map(
        per_device,
        mesh=fine,
        in_specs=(
            P(dp, tensor),
            P(dp, tensor),
            P(dp, tensor),
            P(dp, tensor),
            P(tensor, dp),
            P(dp, tensor, None),
            P(),
        ),
        out_specs=(P(dp, tensor), P(dp, tensor, None), P()),
        check_vma=False,
    )
```
